512 devices in a mesh: seq: 64 (over y, x, core), mp: 8 (over z).
Axes of the slice: x: 4, y: 8, z: 8, core: 2. Of those that a mesh axis runs over, the one named last changes fastest.
Arguments:
- queries: bfloat16 [24576, 2048], P('seq', 'mp')
- neighbor_keys: bfloat16 [98304, 2048], P('seq', 'mp')
- neighbor_values: bfloat16 [98304, 2048], P('seq', 'mp'), may hold values from -6 to 6
- out_grad: bfloat16 [24576, 2048], P('seq', 'mp'), may hold values from -6 to 6
- neighbor_source: int32 [384, 4], P('seq'), may hold values from 0 to 63, as said below
- send_unit: int32 [64, 64, 1], P('seq'), may hold values from -1 to 23, as said below
Outputs:
- attended: bfloat16 [24576, 2048], P('seq', 'mp')
- query_grad: bfloat16 [24576, 2048], P('seq', 'mp')
- key_grad: bfloat16 [98304, 2048], P('seq', 'mp')
- value_grad: bfloat16 [98304, 2048], P('seq', 'mp')
The draws below stay inside these ranges and needn't reach their ends.
Inputs may be any that keep to these rules, and one draw needn't show every extreme that they name: The 24 entries of the groups of one index of seq are distinct, so one owner sends one index at most 1 block; in every draw some owner sends some index 1 block. neighbor_source and send_unit describe the same assignment. `send_unit`: every one of an owner's 24 blocks fills exactly one slot; the other slots hold -1.
All inputs are finite; a program needn't handle non-finite values.
Results may differ from the reference program's by a relative error of at most 0.0072.
Values may be sent and summed in bfloat16 or wider, within the bound.
No kernel may reach another device: no remote copies, remote signals or barrier semaphores. Data moves between devices by JAX's collectives and lax.ppermute only.
A program may use at most 64 MiB of HBM per device.

```python
import jax
import jax.numpy as jnp
from jax import lax

HEADS = 16
HEAD_DIM = 128
GROUP = 64
NEIGHBOURS = 2
SEQ_LEN = 24576
WIDTH = 2048
CH_DEV = 6
UNITS = 24
CAP = 1
TOKENS = 24576
GROUPS = 384
UNIT_ROWS = 98304
N_SEQ = 64


def shuffled_rows(base_key, count, length):

    def one_row(sub_key):
        return jax.random.permutation(sub_key, length)
    return jax.vmap(one_row)(jax.random.split(base_key, count)).astype(jnp.int32)


def assignment(key):
    base = jax.random.fold_in(key, 11)
    owner_perm = jax.random.permutation(jax.random.fold_in(base, 1), N_SEQ).astype(jnp.int32)
    dest_shift = jax.random.permutation(jax.random.fold_in(base, 2), N_SEQ).astype(jnp.int32)
    offset_perm = jax.random.permutation(jax.random.fold_in(base, 3), N_SEQ).astype(jnp.int32)
    slot_order = shuffled_rows(jax.random.fold_in(base, 4), N_SEQ, UNITS)
    unit_order = shuffled_rows(jax.random.fold_in(base, 5), N_SEQ, UNITS)
    counting = jnp.arange(N_SEQ, dtype=jnp.int32)
    owner_inv = jnp.zeros((N_SEQ,), jnp.int32).at[owner_perm].set(counting)
    offset_inv = jnp.zeros((N_SEQ,), jnp.int32).at[offset_perm].set(counting)
    owners = owner_perm[(dest_shift[:, None] + offset_perm[slot_order % N_SEQ]) % N_SEQ]
    source = (owners * CAP + slot_order // N_SEQ).reshape(GROUPS, 2 * NEIGHBOURS)
    first = offset_inv[(owner_inv[:, None] - dest_shift[None, :]) % N_SEQ]
    index = first[:, :, None] + N_SEQ * jnp.arange(CAP, dtype=jnp.int32)[None, None, :]
    valid = index < UNITS
    owner_rows = jnp.broadcast_to(counting[:, None, None], index.shape)
    picked = unit_order[owner_rows, jnp.minimum(index, UNITS - 1)]
    sends = jnp.where(valid, picked, -1).astype(jnp.int32)
    return (source.astype(jnp.int32), sends)


def draw_neighbor_source(key, part):
    return assignment(key)[0]


def draw_send_unit(key, part):
    return assignment(key)[1]


def rough_base(key, rows):
    values = jax.random.normal(jax.random.fold_in(key, 3), (rows, WIDTH), jnp.float32)
    return jnp.clip(values, -6.0, 6.0)


def draw_queries(key, part):
    values = rough_base(jax.random.fold_in(key, 21), TOKENS)
    return values.astype(jnp.bfloat16)


def draw_neighbor_keys(key, part):
    values = rough_base(jax.random.fold_in(key, 31), UNIT_ROWS)
    return values.astype(jnp.bfloat16)


def steps_of(key, extent, pieces, low, high):
    level, own = 1.0, jax.random.fold_in(key, 6)
    for axis_at, parts in pieces:
        draws = jnp.exp(jax.random.uniform(jax.random.fold_in(own, axis_at), (parts,), jnp.float32, low / len(pieces), high / len(pieces)))
        level = level * jnp.repeat(draws, extent[axis_at] // parts).reshape([-1 if axis == axis_at else 1 for axis in range(len(extent))])
    return level


def bell_draw(rng, shape, scale, most, cuts=(), kind=jnp.bfloat16):
    values = jax.random.normal(rng, shape, jnp.float32) * scale
    if len(cuts) > 0:
        values = steps_of(rng, shape, cuts, -0.22, 0.18) * values
    return jnp.clip(values, min=-most, max=most).astype(kind)


def setup_inputs(seed: int = 0) -> dict:
    keys = jax.random.split(jax.random.key(seed), 7)
    queries = draw_queries(jax.random.fold_in(keys[6], 71), 0)
    neighbor_keys = draw_neighbor_keys(jax.random.fold_in(keys[6], 71), 0)
    neighbor_values = bell_draw(keys[2], (UNIT_ROWS, WIDTH), 1.0, 6.0, ((0, 64), (1, 8)))
    out_grad = bell_draw(keys[3], (TOKENS, WIDTH), 1.0, 6.0, ((0, 64), (1, 8)))
    neighbor_source = draw_neighbor_source(jax.random.fold_in(keys[6], 71), 0)
    send_unit = draw_send_unit(jax.random.fold_in(keys[6], 71), 0)
    return {"queries": queries, "neighbor_keys": neighbor_keys, "neighbor_values": neighbor_values, "out_grad": out_grad, "neighbor_source": neighbor_source, "send_unit": send_unit}


def place_back(blocks):
    flat_rows = blocks.reshape(TOKENS, WIDTH)
    front = jnp.zeros((GROUP - 1, WIDTH), jnp.bfloat16)
    return jnp.concatenate([front, flat_rows[:TOKENS - GROUP + 1]], axis=0)


def reference(queries, neighbor_keys, neighbor_values, out_grad, neighbor_source, send_unit):
    score_scale = HEAD_DIM ** -0.5
    per_group = neighbor_source.shape[1]
    owners = neighbor_source // CAP
    cap_slots = neighbor_source % CAP
    devices = jnp.broadcast_to((jnp.arange(GROUPS, dtype=jnp.int32) // CH_DEV)[:, None], neighbor_source.shape)
    local_unit = send_unit[owners, devices, cap_slots]
    unit_ids = jnp.where(local_unit >= 0, owners * UNITS + local_unit, N_SEQ * UNITS).astype(jnp.int32)
    row_ids = (unit_ids[:, :, None] * GROUP + jnp.arange(GROUP, dtype=jnp.int32)[None, None, :]).reshape(GROUPS, per_group * GROUP)
    positions = jnp.arange(TOKENS, dtype=jnp.int32)
    live_rows = jnp.remainder(positions, SEQ_LEN) >= GROUP - 1
    zero_value = jnp.zeros((), jnp.bfloat16)
    live_grad = jnp.where(live_rows[:, None], out_grad, zero_value)
    pad_front = jnp.zeros((1, WIDTH), jnp.bfloat16)
    pad_back = jnp.zeros((GROUP - 1, WIDTH), jnp.bfloat16)
    query_blocks = jnp.concatenate([pad_front, queries, pad_back], axis=0)[GROUP:].reshape(GROUPS, GROUP, WIDTH)
    grad_blocks = jnp.concatenate([pad_front, live_grad, pad_back], axis=0)[GROUP:].reshape(GROUPS, GROUP, WIDTH)
    key_rows = per_group * GROUP

    def one_group(items):
        query_block, grad_block, group_rows = items
        key_block = jnp.take(neighbor_keys, group_rows, axis=0, mode="fill", fill_value=0)
        value_block = jnp.take(neighbor_values, group_rows, axis=0, mode="fill", fill_value=0)
        query_heads = query_block.astype(jnp.float32).reshape(GROUP, HEADS, HEAD_DIM)
        grad_heads = grad_block.astype(jnp.float32).reshape(GROUP, HEADS, HEAD_DIM)
        key_heads = key_block.astype(jnp.float32).reshape(key_rows, HEADS, HEAD_DIM)
        value_heads = value_block.astype(jnp.float32).reshape(key_rows, HEADS, HEAD_DIM)
        scores = jnp.einsum("qhd,khd->hqk", query_heads, key_heads) * score_scale
        row_max = jnp.max(scores, axis=-1, keepdims=True)
        powers = jnp.exp(scores - row_max)
        attn_probs = powers / jnp.sum(powers, axis=-1, keepdims=True)
        probs_low = lax.optimization_barrier(attn_probs.astype(jnp.bfloat16)).astype(jnp.float32)
        mixed_out = jnp.einsum("hqk,khd->qhd", probs_low, value_heads).reshape(GROUP, WIDTH).astype(jnp.bfloat16)
        grad_probs = jnp.einsum("qhd,khd->hqk", grad_heads, value_heads)
        row_dot = jnp.sum(attn_probs * grad_probs, axis=-1, keepdims=True)
        grad_scores = lax.optimization_barrier(((attn_probs * (grad_probs - row_dot)) * score_scale).astype(jnp.bfloat16)).astype(jnp.float32)
        query_part = jnp.einsum("hqk,khd->qhd", grad_scores, key_heads).reshape(GROUP, WIDTH).astype(jnp.bfloat16)
        key_part = jnp.einsum("hqk,qhd->khd", grad_scores, query_heads).reshape(key_rows, WIDTH).astype(jnp.bfloat16)
        value_part = jnp.einsum("hqk,qhd->khd", probs_low, grad_heads).reshape(key_rows, WIDTH).astype(jnp.bfloat16)
        return mixed_out, query_part, key_part, value_part

    mixed_out, query_part, key_part, value_part = lax.map(one_group, (query_blocks, grad_blocks, row_ids))
    attended = jnp.where(live_rows[:, None], place_back(mixed_out), zero_value)
    query_grad = place_back(query_part)
    flat_ids = row_ids.reshape(-1)
    key_grad = jnp.zeros((UNIT_ROWS, WIDTH), jnp.bfloat16).at[flat_ids].add(key_part.reshape(-1, WIDTH), mode="drop")
    value_grad = jnp.zeros((UNIT_ROWS, WIDTH), jnp.bfloat16).at[flat_ids].add(value_part.reshape(-1, WIDTH), mode="drop")
    return attended, query_grad, key_grad, value_grad
```

```python
import functools

import jax
import jax.numpy as jnp
from jax import lax
from jax.experimental import pallas as pl
from jax.experimental.pallas import tpu as pltpu
from jax.sharding import PartitionSpec as P

HEAD_DIM = 128
GROUP = 64
VMEM_LIMIT = 24 * 1024 * 1024
SCALE = HEAD_DIM ** (-0.5)

VM = pl.BlockSpec(memory_space=pltpu.VMEM)
SM = pl.BlockSpec(memory_space=pltpu.SMEM)


def call(kernel, out_shape, n_smem, n_vmem, flops=0, moved=0, scratch=()):
    return pl.pallas_call(
        kernel,
        out_shape=out_shape,
        in_specs=[SM] * n_smem + [VM] * n_vmem,
        out_specs=jax.tree.map(lambda _: VM, out_shape),
        scratch_shapes=list(scratch),
        compiler_params=pltpu.CompilerParams(vmem_limit_bytes=VMEM_LIMIT),
        cost_estimate=pl.CostEstimate(flops=flops, bytes_accessed=moved, transcendentals=0),
    )


def pack_kernel(table, units, slots):
    def body(slot, carry):
        unit = table[slot]

        @pl.when(unit >= 0)
        def _():
            slots[slot] = units[unit]

        @pl.when(unit < 0)
        def _():
            slots[slot] = jnp.zeros(slots.shape[1:], slots.dtype)

        return carry

    lax.fori_loop(0, slots.shape[0], body, 0)


def unpack_kernel(table, slots, units):
    units[...] = jnp.zeros(units.shape, units.dtype)

    def body(slot, carry):
        unit = table[slot]

        @pl.when(unit >= 0)
        def _():
            units[unit] = slots[slot]

        return carry

    lax.fori_loop(0, slots.shape[0], body, 0)


def dot(a, b, contract):
    return lax.dot_general(a, b, ((contract[:1], contract[1:]), ((), ())), preferred_element_type=jnp.float32)


def gather_group(source, slots, group, per_group):
    return jnp.concatenate([slots[source[group * per_group + j]] for j in range(per_group)], axis=0)


def scatter_group(source, slots, group, per_group, column, part):
    for j in range(per_group):
        slots[source[group * per_group + j], :, column] = part[j * GROUP : (j + 1) * GROUP]


def probs_kernel(per_group, source, queries, grads, keys, probs, value_send):
    value_send[...] = jnp.zeros(value_send.shape, value_send.dtype)

    def body(group, carry):
        rows = pl.ds(pl.multiple_of(group * GROUP, GROUP), GROUP)
        key_block = gather_group(source, keys, group, per_group)
        for head in range(queries.shape[1] // HEAD_DIM):
            column = slice(head * HEAD_DIM, (head + 1) * HEAD_DIM)
            scores = dot(queries[rows, column], key_block[:, column], (1, 1)) * SCALE
            powers = jnp.exp(scores - jnp.max(scores, axis=-1, keepdims=True))
            chances = powers / jnp.sum(powers, axis=-1, keepdims=True)
            probs[group, head] = chances
            value_part = dot(chances.astype(jnp.bfloat16), grads[rows, column], (0, 0))
            scatter_group(source, value_send, group, per_group, column, value_part.astype(jnp.bfloat16))
        return carry

    lax.fori_loop(0, probs.shape[0], body, 0)


def grads_kernel(per_group, source, queries, grads, probs, keys, values, attended, query_grad, key_send):
    key_send[...] = jnp.zeros(key_send.shape, key_send.dtype)

    def body(group, carry):
        rows = pl.ds(pl.multiple_of(group * GROUP, GROUP), GROUP)
        key_block = gather_group(source, keys, group, per_group)
        value_block = gather_group(source, values, group, per_group)
        for head in range(queries.shape[1] // HEAD_DIM):
            column = slice(head * HEAD_DIM, (head + 1) * HEAD_DIM)
            chances = probs[group, head]
            mixed = dot(chances.astype(jnp.bfloat16), value_block[:, column], (1, 0))
            attended[rows, column] = mixed.astype(jnp.bfloat16)
            grad_probs = dot(grads[rows, column], value_block[:, column], (1, 1))
            row_dot = jnp.sum(chances * grad_probs, axis=-1, keepdims=True)
            grad_scores = (chances * (grad_probs - row_dot) * SCALE).astype(jnp.bfloat16)
            query_part = dot(grad_scores, key_block[:, column], (1, 0))
            query_grad[rows, column] = query_part.astype(jnp.bfloat16)
            key_part = dot(grad_scores, queries[rows, column], (0, 0))
            scatter_group(source, key_send, group, per_group, column, key_part.astype(jnp.bfloat16))
        return carry

    lax.fori_loop(0, probs.shape[0], body, 0)


def shift(value, axis, steps):
    count = lax.axis_size(axis)
    first, last = max(0, -steps), min(count, count - steps)
    return lax.ppermute(value, axis, [(at, at + steps) for at in range(first, last)])


def exchange(slots):
    return lax.all_to_all(slots, "seq", split_axis=0, concat_axis=0, tiled=True)


def local(queries, neighbor_keys, neighbor_values, out_grad, neighbor_source, send_unit):
    tok_rows, cols = queries.shape
    groups, per_group = neighbor_source.shape
    units = neighbor_keys.shape[0] // GROUP
    slots = send_unit.shape[1] * send_unit.shape[2]
    heads = cols // HEAD_DIM
    low = jnp.bfloat16
    table = send_unit.reshape(slots)
    source = neighbor_source.reshape(units)
    slot_shape = jax.ShapeDtypeStruct((slots, GROUP, cols), low)
    unit_shape = jax.ShapeDtypeStruct((units, GROUP, cols), low)
    tok_shape = jax.ShapeDtypeStruct((tok_rows, cols), low)
    slot_bytes = slots * GROUP * cols * 2
    pack = call(pack_kernel, slot_shape, 1, 1, moved=2 * slot_bytes)
    unpack = call(unpack_kernel, unit_shape, 1, 1, moved=2 * slot_bytes)
    matmul = 2 * tok_rows * cols * per_group * GROUP

    key_slots = exchange(pack(table, neighbor_keys.reshape(unit_shape.shape)))
    value_slots = exchange(pack(table, neighbor_values.reshape(unit_shape.shape)))

    edge = GROUP - 1
    ahead = shift(jnp.stack([queries[:GROUP], out_grad[:GROUP]]), "seq", -1)
    group_queries = jnp.concatenate([queries[edge:], ahead[0, :edge]], axis=0)
    group_grads = jnp.concatenate([out_grad[edge:], ahead[1, :edge]], axis=0)

    probs, value_send = call(
        functools.partial(probs_kernel, per_group),
        (jax.ShapeDtypeStruct((groups, heads, GROUP, per_group * GROUP), jnp.float32), slot_shape),
        1, 3, flops=2 * matmul, moved=2 * slot_bytes,
    )(source, group_queries, group_grads, key_slots)
    value_back = exchange(value_send)
    mixed, query_part, key_send = call(
        functools.partial(grads_kernel, per_group),
        (tok_shape, tok_shape, slot_shape),
        1, 5, flops=4 * matmul, moved=3 * slot_bytes,
    )(source, group_queries, group_grads, probs, key_slots, value_slots)
    key_back = exchange(key_send)

    behind = shift(jnp.stack([mixed[-GROUP:], query_part[-GROUP:]]), "seq", 1)
    attended = jnp.concatenate([behind[0, 1:], mixed[: tok_rows - edge]], axis=0)
    query_grad = jnp.concatenate([behind[1, 1:], query_part[: tok_rows - edge]], axis=0)
    value_grad = unpack(table, value_back).reshape(units * GROUP, cols)
    key_grad = unpack(table, key_back).reshape(units * GROUP, cols)
    return (attended, query_grad, key_grad, value_grad)


def solution(mesh):
    return jax.shard_map(
        local,
        mesh=mesh,
        in_specs=(
            P("seq", "mp"),
            P("seq", "mp"),
            P("seq", "mp"),
            P("seq", "mp"),
            P("seq", None),
            P("seq", None, None),
        ),
        out_specs=(P("seq", "mp"), P("seq", "mp"), P("seq", "mp"), P("seq", "mp")),
        check_vma=False,
    )
```

```python
import functools

import jax
import jax.numpy as jnp
from jax import lax
from jax.experimental import pallas as pl
from jax.experimental.pallas import tpu as pltpu
from jax.sharding import PartitionSpec as P

HEAD_DIM = 128
GROUP = 64
PAIR = 2 * GROUP
VMEM_LIMIT = 58 * 1024 * 1024
SCALE = HEAD_DIM ** (-0.5)

VM = pl.BlockSpec(memory_space=pltpu.VMEM)
SM = pl.BlockSpec(memory_space=pltpu.SMEM)
HB = pl.BlockSpec(memory_space=pltpu.HBM)


def call(kernel, in_specs, out_specs, out_shape, scratch=(), flops=0, moved=0):
    return pl.pallas_call(
        kernel,
        out_shape=out_shape,
        in_specs=in_specs,
        out_specs=out_specs,
        scratch_shapes=list(scratch),
        compiler_params=pltpu.CompilerParams(vmem_limit_bytes=VMEM_LIMIT),
        cost_estimate=pl.CostEstimate(flops=flops, bytes_accessed=moved, transcendentals=0),
    )


def pack_kernel(table, keys, values, slots, zeros, sem):
    zeros[...] = jnp.zeros(zeros.shape, zeros.dtype)

    def body(slot, carry):
        unit = table[slot]

        @pl.when(unit >= 0)
        def _():
            pltpu.make_async_copy(keys.at[unit], slots.at[slot, pl.ds(0, GROUP)], sem).start()
            pltpu.make_async_copy(values.at[unit], slots.at[slot, pl.ds(GROUP, GROUP)], sem).start()

        @pl.when(unit < 0)
        def _():
            pltpu.make_async_copy(zeros, slots.at[slot], sem).start()

        return carry

    lax.fori_loop(0, slots.shape[0], body, 0)
    pltpu.make_async_copy(slots, slots, sem).wait()


def unpack_kernel(which, slots, keys, values, zeros, key_sem, value_sem):
    zeros[...] = jnp.zeros(zeros.shape, zeros.dtype)

    def body(unit, carry):
        slot = which[unit]

        @pl.when(slot >= 0)
        def _():
            pltpu.make_async_copy(slots.at[slot, pl.ds(0, GROUP)], keys.at[unit], key_sem).start()
            pltpu.make_async_copy(slots.at[slot, pl.ds(GROUP, GROUP)], values.at[unit], value_sem).start()

        @pl.when(slot < 0)
        def _():
            pltpu.make_async_copy(zeros, keys.at[unit], key_sem).start()
            pltpu.make_async_copy(zeros, values.at[unit], value_sem).start()

        return carry

    lax.fori_loop(0, keys.shape[0], body, 0)
    pltpu.make_async_copy(keys, keys, key_sem).wait()
    pltpu.make_async_copy(values, values, value_sem).wait()


def dot(a, b, contract):
    return lax.dot_general(a, b, ((contract[:1], contract[1:]), ((), ())), preferred_element_type=jnp.float32)


def by_head(rows):
    blank = jnp.zeros((rows.shape[0], HEAD_DIM), rows.dtype)
    heads = rows.shape[1] // HEAD_DIM
    return jnp.concatenate(
        [
            jnp.concatenate(
                [rows[:, h * HEAD_DIM : (h + 1) * HEAD_DIM] if h == at else blank for h in range(heads)], axis=1
            )
            for at in range(heads)
        ],
        axis=0,
    )


def block_kernel(
    source, queries, grads, slots, send, probs, scores_grad, blocks, block_grads, zeros, in_sems, zero_sem, out_sem
):
    groups, per_group = blocks.shape[:2]
    keys, cols = per_group * GROUP, blocks.shape[3]
    low = jnp.bfloat16
    for group in range(groups):
        for j in range(per_group):
            slot = source[group * per_group + j]
            pltpu.make_async_copy(slots.at[slot], blocks.at[group, j], in_sems.at[group]).start()
    zeros[...] = jnp.zeros(zeros.shape, low)
    many = zeros.shape[0]
    for first in range(0, send.shape[0], many):
        pltpu.make_async_copy(zeros, send.at[pl.ds(first, many)], zero_sem).start()
    for group in range(groups):
        pltpu.make_async_copy(blocks.at[group], blocks.at[group], in_sems.at[group]).wait()
        rows = slice(group * GROUP, (group + 1) * GROUP)
        query = by_head(queries[rows])
        grad = by_head(grads[rows])
        key = blocks[group, :, :GROUP].reshape(keys, cols)
        value = blocks[group, :, GROUP:].reshape(keys, cols)
        scores = dot(key, query, (1, 1)) * SCALE
        powers = jnp.exp(scores - jnp.max(scores, axis=0, keepdims=True))
        chances = powers * (1.0 / jnp.sum(powers, axis=0, keepdims=True))
        chances_low = chances.astype(low)
        probs[group] = chances_low
        value_part = dot(chances_low, grad, (1, 0)).astype(low)
        block_grads[group, :, GROUP:] = value_part.reshape(per_group, GROUP, cols)
        grad_probs = dot(value, grad, (1, 1))
        row_dot = jnp.sum(chances * grad_probs, axis=0, keepdims=True)
        grad_low = (chances * (grad_probs - row_dot) * SCALE).astype(low)
        scores_grad[group] = grad_low
        key_part = dot(grad_low, query, (1, 0)).astype(low)
        block_grads[group, :, :GROUP] = key_part.reshape(per_group, GROUP, cols)
        if group == 0:
            pltpu.make_async_copy(send, send, zero_sem).wait()
        for j in range(per_group):
            slot = source[group * per_group + j]
            pltpu.make_async_copy(block_grads.at[group, j], send.at[slot], out_sem).start()
    pltpu.make_async_copy(block_grads, block_grads, out_sem).wait()


def token_kernel(source, probs, scores_grad, slots, attended, query_grad, blocks, in_sems):
    groups, per_group = blocks.shape[:2]
    keys, cols = per_group * GROUP, blocks.shape[3]
    for group in range(groups):
        for j in range(per_group):
            slot = source[group * per_group + j]
            pltpu.make_async_copy(slots.at[slot], blocks.at[group, j], in_sems.at[group]).start()
    for group in range(groups):
        pltpu.make_async_copy(blocks.at[group], blocks.at[group], in_sems.at[group]).wait()
        rows = slice(group * GROUP, (group + 1) * GROUP)
        key = blocks[group, :, :GROUP].reshape(keys, cols)
        value = blocks[group, :, GROUP:].reshape(keys, cols)
        mixed = dot(probs[group], value, (0, 0)).astype(jnp.bfloat16)
        query_part = dot(scores_grad[group], key, (0, 0)).astype(jnp.bfloat16)
        for head in range(cols // HEAD_DIM):
            own = slice(head * GROUP, (head + 1) * GROUP)
            column = slice(head * HEAD_DIM, (head + 1) * HEAD_DIM)
            attended[rows, column] = mixed[own, column]
            query_grad[rows, column] = query_part[own, column]


def shift(value, axis, steps):
    count = lax.axis_size(axis)
    first, last = max(0, -steps), min(count, count - steps)
    return lax.ppermute(value, axis, [(at, at + steps) for at in range(first, last)])


def exchange(slots):
    return lax.all_to_all(slots, "seq", split_axis=0, concat_axis=0, tiled=True)


def local(queries, neighbor_keys, neighbor_values, out_grad, neighbor_source, send_unit):
    tok_rows, cols = queries.shape
    groups, per_group = neighbor_source.shape
    units = neighbor_keys.shape[0] // GROUP
    slots = send_unit.shape[1] * send_unit.shape[2]
    heads, keys = cols // HEAD_DIM, per_group * GROUP
    low = jnp.bfloat16
    table = send_unit.reshape(slots)
    source = neighbor_source.reshape(units)
    slot_shape = jax.ShapeDtypeStruct((slots, PAIR, cols), low)
    unit_shape = jax.ShapeDtypeStruct((units, GROUP, cols), low)
    tok_shape = jax.ShapeDtypeStruct((tok_rows, cols), low)
    prob_shape = jax.ShapeDtypeStruct((groups, keys, heads * GROUP), low)
    slot_bytes = slots * PAIR * cols * 2
    matmul = 2 * groups * keys * heads * GROUP * cols
    blocks = pltpu.VMEM((groups, per_group, PAIR, cols), low)
    group_sems = pltpu.SemaphoreType.DMA((groups,))

    received = exchange(
        call(
            pack_kernel, [SM, HB, HB], HB, slot_shape,
            scratch=[pltpu.VMEM((PAIR, cols), low), pltpu.SemaphoreType.DMA],
            moved=2 * slot_bytes,
        )(table, neighbor_keys.reshape(unit_shape.shape), neighbor_values.reshape(unit_shape.shape))
    )

    edge = GROUP - 1
    ahead = shift(jnp.stack([queries[:GROUP], out_grad[:GROUP]]), "seq", -1)
    group_queries = jnp.concatenate([queries[edge:], ahead[0, :edge]], axis=0)
    group_grads = jnp.concatenate([out_grad[edge:], ahead[1, :edge]], axis=0)
    fills = table[None, :] == jnp.arange(units, dtype=jnp.int32)[:, None]
    which = jnp.max(jnp.where(fills, jnp.arange(slots, dtype=jnp.int32)[None, :], -1), axis=1)

    send, probs, scores_grad = call(
        block_kernel, [SM, VM, VM, HB], (HB, VM, VM), (slot_shape, prob_shape, prob_shape),
        scratch=[
            blocks, blocks, pltpu.VMEM((8, PAIR, cols), low),
            group_sems, pltpu.SemaphoreType.DMA, pltpu.SemaphoreType.DMA,
        ],
        flops=4 * matmul, moved=slot_bytes,
    )(source, group_queries, group_grads, received)
    returned = exchange(send)

    mixed, query_part = call(
        token_kernel, [SM, VM, VM, HB], (VM, VM), (tok_shape, tok_shape),
        scratch=[blocks, group_sems], flops=2 * matmul, moved=slot_bytes,
    )(source, probs, scores_grad, received)
    behind = shift(jnp.stack([mixed[-GROUP:], query_part[-GROUP:]]), "seq", 1)
    attended = jnp.concatenate([behind[0, 1:], mixed[: tok_rows - edge]], axis=0)
    query_grad = jnp.concatenate([behind[1, 1:], query_part[: tok_rows - edge]], axis=0)

    key_grad, value_grad = call(
        unpack_kernel, [SM, HB], (HB, HB), (unit_shape, unit_shape),
        scratch=[pltpu.VMEM((GROUP, cols), low), pltpu.SemaphoreType.DMA, pltpu.SemaphoreType.DMA],
        moved=slot_bytes,
    )(which, returned)
    flat = (units * GROUP, cols)
    return (attended, query_grad, key_grad.reshape(flat), value_grad.reshape(flat))


def solution(mesh):
    return jax.shard_map(
        local,
        mesh=mesh,
        in_specs=(
            P("seq", "mp"),
            P("seq", "mp"),
            P("seq", "mp"),
            P("seq", "mp"),
            P("seq", None),
            P("seq", None, None),
        ),
        out_specs=(P("seq", "mp"), P("seq", "mp"), P("seq", "mp"), P("seq", "mp")),
        check_vma=False,
    )
```

```python
import functools

import jax
import jax.numpy as jnp
from jax import lax
from jax.experimental import pallas as pl
from jax.experimental.pallas import tpu as pltpu
from jax.sharding import PartitionSpec as P

HEAD_DIM = 128
GROUP = 64
PAIR = 2 * GROUP
VMEM_LIMIT = 58 * 1024 * 1024
SCALE = HEAD_DIM ** (-0.5)

VM = pl.BlockSpec(memory_space=pltpu.VMEM)
SM = pl.BlockSpec(memory_space=pltpu.SMEM)
HB = pl.BlockSpec(memory_space=pltpu.HBM)


def call(kernel, in_specs, out_specs, out_shape, scratch=(), flops=0, moved=0):
    return pl.pallas_call(
        kernel,
        out_shape=out_shape,
        in_specs=in_specs,
        out_specs=out_specs,
        scratch_shapes=list(scratch),
        compiler_params=pltpu.CompilerParams(vmem_limit_bytes=VMEM_LIMIT),
        cost_estimate=pl.CostEstimate(flops=flops, bytes_accessed=moved, transcendentals=0),
    )


def pack_kernel(table, keys, values, slots, staged, zeros, in_sem, out_sem):
    loads = [
        pltpu.make_async_copy(keys, staged.at[:, pl.ds(0, GROUP)], in_sem.at[0]),
        pltpu.make_async_copy(values, staged.at[:, pl.ds(GROUP, GROUP)], in_sem.at[1]),
    ]
    for load in loads:
        load.start()
    zeros[...] = jnp.zeros(zeros.shape, zeros.dtype)

    def blank(slot, carry):
        @pl.when(table[slot] < 0)
        def _():
            pltpu.make_async_copy(zeros, slots.at[slot], out_sem).start()

        return carry

    def fill(slot, carry):
        unit = table[slot]

        @pl.when(unit >= 0)
        def _():
            pltpu.make_async_copy(staged.at[unit], slots.at[slot], out_sem).start()

        return carry

    lax.fori_loop(0, slots.shape[0], blank, 0)
    for load in loads:
        load.wait()
    lax.fori_loop(0, slots.shape[0], fill, 0)
    pltpu.make_async_copy(slots, slots, out_sem).wait()


def unpack_kernel(which, slots, keys, values, staged, zeros, in_sems, key_sem, value_sem):
    zeros[...] = jnp.zeros(zeros.shape, zeros.dtype)
    parts = in_sems.shape[0]
    some = keys.shape[0] // parts

    def body(unit, carry):
        slot = which[unit]
        sem = in_sems.at[unit // some]

        @pl.when(slot >= 0)
        def _():
            pltpu.make_async_copy(slots.at[slot], staged.at[unit], sem).start()

        @pl.when(slot < 0)
        def _():
            pltpu.make_async_copy(zeros, staged.at[unit], sem).start()

        return carry

    lax.fori_loop(0, keys.shape[0], body, 0)
    for part in range(parts):
        own = pl.ds(part * some, some)
        pltpu.make_async_copy(staged.at[own], staged.at[own], in_sems.at[part]).wait()
        pltpu.make_async_copy(staged.at[own, pl.ds(0, GROUP)], keys.at[own], key_sem).start()
        pltpu.make_async_copy(staged.at[own, pl.ds(GROUP, GROUP)], values.at[own], value_sem).start()
    pltpu.make_async_copy(keys, keys, key_sem).wait()
    pltpu.make_async_copy(values, values, value_sem).wait()


def dot(a, b, contract):
    return lax.dot_general(a, b, ((contract[:1], contract[1:]), ((), ())), preferred_element_type=jnp.float32)


def by_head(rows):
    blank = jnp.zeros((rows.shape[0], HEAD_DIM), rows.dtype)
    heads = rows.shape[1] // HEAD_DIM
    return jnp.concatenate(
        [
            jnp.concatenate(
                [rows[:, h * HEAD_DIM : (h + 1) * HEAD_DIM] if h == at else blank for h in range(heads)], axis=1
            )
            for at in range(heads)
        ],
        axis=0,
    )


def block_kernel(
    source, queries, grads, slots, send, probs, scores_grad, blocks, block_grads, zeros, in_sems, zero_sem, out_sem
):
    groups, per_group = blocks.shape[:2]
    keys, cols = per_group * GROUP, blocks.shape[3]
    low = jnp.bfloat16
    for group in range(groups):
        for j in range(per_group):
            slot = source[group * per_group + j]
            pltpu.make_async_copy(slots.at[slot], blocks.at[group, j], in_sems.at[group]).start()
    zeros[...] = jnp.zeros(zeros.shape, low)
    many = zeros.shape[0]
    for first in range(0, send.shape[0], many):
        pltpu.make_async_copy(zeros, send.at[pl.ds(first, many)], zero_sem).start()
    for group in range(groups):
        pltpu.make_async_copy(blocks.at[group], blocks.at[group], in_sems.at[group]).wait()
        rows = slice(group * GROUP, (group + 1) * GROUP)
        query = by_head(queries[rows])
        grad = by_head(grads[rows])
        key = blocks[group, :, :GROUP].reshape(keys, cols)
        value = blocks[group, :, GROUP:].reshape(keys, cols)
        scores = dot(key, query, (1, 1)) * SCALE
        powers = jnp.exp(scores - jnp.max(scores, axis=0, keepdims=True))
        chances = powers * (1.0 / jnp.sum(powers, axis=0, keepdims=True))
        chances_low = chances.astype(low)
        probs[group] = chances_low
        value_part = dot(chances_low, grad, (1, 0)).astype(low)
        block_grads[group, :, GROUP:] = value_part.reshape(per_group, GROUP, cols)
        grad_probs = dot(value, grad, (1, 1))
        row_dot = jnp.sum(chances * grad_probs, axis=0, keepdims=True)
        grad_low = (chances * (grad_probs - row_dot) * SCALE).astype(low)
        scores_grad[group] = grad_low
        key_part = dot(grad_low, query, (1, 0)).astype(low)
        block_grads[group, :, :GROUP] = key_part.reshape(per_group, GROUP, cols)
        if group == 0:
            pltpu.make_async_copy(send, send, zero_sem).wait()
        for j in range(per_group):
            slot = source[group * per_group + j]
            pltpu.make_async_copy(block_grads.at[group, j], send.at[slot], out_sem).start()
    pltpu.make_async_copy(block_grads, block_grads, out_sem).wait()


def token_kernel(source, probs, scores_grad, slots, attended, query_grad, blocks, in_sems):
    groups, per_group = blocks.shape[:2]
    keys, cols = per_group * GROUP, blocks.shape[3]
    for group in range(groups):
        for j in range(per_group):
            slot = source[group * per_group + j]
            pltpu.make_async_copy(slots.at[slot], blocks.at[group, j], in_sems.at[group]).start()
    for group in range(groups):
        pltpu.make_async_copy(blocks.at[group], blocks.at[group], in_sems.at[group]).wait()
        rows = slice(group * GROUP, (group + 1) * GROUP)
        key = blocks[group, :, :GROUP].reshape(keys, cols)
        value = blocks[group, :, GROUP:].reshape(keys, cols)
        mixed = dot(probs[group], value, (0, 0)).astype(jnp.bfloat16)
        query_part = dot(scores_grad[group], key, (0, 0)).astype(jnp.bfloat16)
        for head in range(cols // HEAD_DIM):
            own = slice(head * GROUP, (head + 1) * GROUP)
            column = slice(head * HEAD_DIM, (head + 1) * HEAD_DIM)
            attended[rows, column] = mixed[own, column]
            query_grad[rows, column] = query_part[own, column]


def shift(value, axis, steps):
    count = lax.axis_size(axis)
    first, last = max(0, -steps), min(count, count - steps)
    return lax.ppermute(value, axis, [(at, at + steps) for at in range(first, last)])


def exchange(slots):
    return lax.all_to_all(slots, "seq", split_axis=0, concat_axis=0, tiled=True)


def local(queries, neighbor_keys, neighbor_values, out_grad, neighbor_source, send_unit):
    tok_rows, cols = queries.shape
    groups, per_group = neighbor_source.shape
    units = neighbor_keys.shape[0] // GROUP
    slots = send_unit.shape[1] * send_unit.shape[2]
    heads, keys = cols // HEAD_DIM, per_group * GROUP
    low = jnp.bfloat16
    table = send_unit.reshape(slots)
    source = neighbor_source.reshape(units)
    slot_shape = jax.ShapeDtypeStruct((slots, PAIR, cols), low)
    unit_shape = jax.ShapeDtypeStruct((units, GROUP, cols), low)
    tok_shape = jax.ShapeDtypeStruct((tok_rows, cols), low)
    prob_shape = jax.ShapeDtypeStruct((groups, keys, heads * GROUP), low)
    slot_bytes = slots * PAIR * cols * 2
    matmul = 2 * groups * keys * heads * GROUP * cols
    blocks = pltpu.VMEM((groups, per_group, PAIR, cols), low)
    staged = pltpu.VMEM((units, PAIR, cols), low)
    group_sems = pltpu.SemaphoreType.DMA((groups,))

    received = exchange(
        call(
            pack_kernel, [SM, HB, HB], HB, slot_shape,
            scratch=[
                staged, pltpu.VMEM((PAIR, cols), low),
                pltpu.SemaphoreType.DMA((2,)), pltpu.SemaphoreType.DMA,
            ],
            moved=2 * slot_bytes,
        )(table, neighbor_keys.reshape(unit_shape.shape), neighbor_values.reshape(unit_shape.shape))
    )

    edge = GROUP - 1
    ahead = shift(jnp.stack([queries[:GROUP], out_grad[:GROUP]]), "seq", -1)
    group_queries = jnp.concatenate([queries[edge:], ahead[0, :edge]], axis=0)
    group_grads = jnp.concatenate([out_grad[edge:], ahead[1, :edge]], axis=0)
    fills = table[None, :] == jnp.arange(units, dtype=jnp.int32)[:, None]
    which = jnp.max(jnp.where(fills, jnp.arange(slots, dtype=jnp.int32)[None, :], -1), axis=1)

    send, probs, scores_grad = call(
        block_kernel, [SM, VM, VM, HB], (HB, VM, VM), (slot_shape, prob_shape, prob_shape),
        scratch=[
            blocks, blocks, pltpu.VMEM((8, PAIR, cols), low),
            group_sems, pltpu.SemaphoreType.DMA, pltpu.SemaphoreType.DMA,
        ],
        flops=4 * matmul, moved=slot_bytes,
    )(source, group_queries, group_grads, received)
    returned = exchange(send)

    mixed, query_part = call(
        token_kernel, [SM, VM, VM, HB], (VM, VM), (tok_shape, tok_shape),
        scratch=[blocks, group_sems], flops=2 * matmul, moved=slot_bytes,
    )(source, probs, scores_grad, received)
    behind = shift(jnp.stack([mixed[-GROUP:], query_part[-GROUP:]]), "seq", 1)
    attended = jnp.concatenate([behind[0, 1:], mixed[: tok_rows - edge]], axis=0)
    query_grad = jnp.concatenate([behind[1, 1:], query_part[: tok_rows - edge]], axis=0)

    key_grad, value_grad = call(
        unpack_kernel, [SM, HB], (HB, HB), (unit_shape, unit_shape),
        scratch=[
            staged, pltpu.VMEM((PAIR, cols), low),
            pltpu.SemaphoreType.DMA((4,)), pltpu.SemaphoreType.DMA, pltpu.SemaphoreType.DMA,
        ],
        moved=slot_bytes,
    )(which, returned)
    flat = (units * GROUP, cols)
    return (attended, query_grad, key_grad.reshape(flat), value_grad.reshape(flat))


def solution(mesh):
    return jax.shard_map(
        local,
        mesh=mesh,
        in_specs=(
            P("seq", "mp"),
            P("seq", "mp"),
            P("seq", "mp"),
            P("seq", "mp"),
            P("seq", None),
            P("seq", None, None),
        ),
        out_specs=(P("seq", "mp"), P("seq", "mp"), P("seq", "mp"), P("seq", "mp")),
        check_vma=False,
    )
```

```python
import jax
import jax.numpy as jnp
from jax import lax
from jax.experimental import pallas as pl
from jax.experimental.pallas import tpu as pltpu
from jax.sharding import PartitionSpec as P

HEAD_DIM = 128
GROUP = 64
PAIR = 2 * GROUP
MIB = 1024 * 1024
SCALE = HEAD_DIM ** (-0.5)
SIDE = 3

VM = pl.BlockSpec(memory_space=pltpu.VMEM)
SM = pl.BlockSpec(memory_space=pltpu.SMEM)
HB = pl.BlockSpec(memory_space=pltpu.HBM)


def call(kernel, in_specs, out_specs, out_shape, scratch=(), flops=0, moved=0, aliases=None, vmem=12):
    return pl.pallas_call(
        kernel,
        out_shape=out_shape,
        in_specs=in_specs,
        out_specs=out_specs,
        scratch_shapes=list(scratch),
        input_output_aliases=aliases or {},
        compiler_params=pltpu.CompilerParams(vmem_limit_bytes=vmem * MIB),
        cost_estimate=pl.CostEstimate(flops=flops, bytes_accessed=moved, transcendentals=0),
    )


def blank_kernel(slots, zeros, sem):
    zeros[...] = jnp.zeros(zeros.shape, zeros.dtype)
    many = zeros.shape[0]
    for first in range(0, slots.shape[0], many):
        pltpu.make_async_copy(zeros, slots.at[pl.ds(first, many)], sem).start()
    pltpu.make_async_copy(slots, slots, sem).wait()


def pack_kernel(table, keys, values, slots, staged, zeros, in_sems, out_sem):
    parts = in_sems.shape[0]
    some = keys.shape[0] // parts
    loads = []
    for part in range(parts):
        own = pl.ds(part * some, some)
        loads.append(pltpu.make_async_copy(keys.at[own], staged.at[own, pl.ds(0, GROUP)], in_sems.at[part, 0]))
        loads.append(pltpu.make_async_copy(values.at[own], staged.at[own, pl.ds(GROUP, GROUP)], in_sems.at[part, 1]))
    for load in loads:
        load.start()
    zeros[...] = jnp.zeros(zeros.shape, zeros.dtype)
    for slot in range(slots.shape[0]):

        @pl.when(table[slot] < 0)
        def _():
            pltpu.make_async_copy(zeros, slots.at[slot], out_sem).start()

    for load in loads:
        load.wait()
    for slot in range(slots.shape[0]):
        unit = table[slot]

        @pl.when(unit >= 0)
        def _():
            pltpu.make_async_copy(staged.at[unit], slots.at[slot], out_sem).start()

    pltpu.make_async_copy(slots, slots, out_sem).wait()


def unpack_kernel(which, slots, keys, values, staged, zeros, in_sems, key_sem, value_sem):
    zeros[...] = jnp.zeros(zeros.shape, zeros.dtype)
    parts = in_sems.shape[0]
    some = keys.shape[0] // parts
    for unit in range(keys.shape[0]):
        slot = which[unit]

        @pl.when(slot >= 0)
        def _():
            pltpu.make_async_copy(slots.at[slot], staged.at[unit], in_sems.at[unit // some]).start()

        @pl.when(slot < 0)
        def _():
            pltpu.make_async_copy(zeros, staged.at[unit], in_sems.at[unit // some]).start()

    for part in range(parts):
        own = pl.ds(part * some, some)
        pltpu.make_async_copy(staged.at[own], staged.at[own], in_sems.at[part]).wait()
        pltpu.make_async_copy(staged.at[own, pl.ds(0, GROUP)], keys.at[own], key_sem).start()
        pltpu.make_async_copy(staged.at[own, pl.ds(GROUP, GROUP)], values.at[own], value_sem).start()
    pltpu.make_async_copy(keys, keys, key_sem).wait()
    pltpu.make_async_copy(values, values, value_sem).wait()


def dot(a, b, contract):
    return lax.dot_general(a, b, ((contract[:1], contract[1:]), ((), ())), preferred_element_type=jnp.float32)


def by_head(rows):
    blank = jnp.zeros((rows.shape[0], HEAD_DIM), rows.dtype)
    heads = rows.shape[1] // HEAD_DIM
    return jnp.concatenate(
        [
            jnp.concatenate(
                [rows[:, h * HEAD_DIM : (h + 1) * HEAD_DIM] if h == at else blank for h in range(heads)], axis=1
            )
            for at in range(heads)
        ],
        axis=0,
    )


def gather(source, slots, blocks, sems):
    groups, per_group = blocks.shape[:2]
    for group in range(groups):
        for j in range(per_group):
            slot = source[group * per_group + j]
            pltpu.make_async_copy(slots.at[slot], blocks.at[group, j], sems.at[group]).start()


def half(blocks, group, part):
    per_group, _, cols = blocks.shape[1:]
    return blocks[group, :, part * GROUP : (part + 1) * GROUP].reshape(per_group * GROUP, cols)


def block_kernel(
    source, queries, grads, slots, blank, send, probs, scores_grad, blocks, block_grads, in_sems, out_sem
):
    groups, per_group, _, cols = blocks.shape
    low = jnp.bfloat16
    gather(source, slots, blocks, in_sems)
    for first in range(0, groups, SIDE):
        side = range(first, min(first + SIDE, groups))
        query = [by_head(queries[g * GROUP : (g + 1) * GROUP]) for g in side]
        grad = [by_head(grads[g * GROUP : (g + 1) * GROUP]) for g in side]
        for g in side:
            pltpu.make_async_copy(blocks.at[g], blocks.at[g], in_sems.at[g]).wait()
        scores = [dot(half(blocks, g, 0), q, (1, 1)) * SCALE for g, q in zip(side, query)]
        grad_probs = [dot(half(blocks, g, 1), d, (1, 1)) for g, d in zip(side, grad)]
        powers = [jnp.exp(s - jnp.max(s, axis=0, keepdims=True)) for s in scores]
        chances = [p * (1.0 / jnp.sum(p, axis=0, keepdims=True)) for p in powers]
        chances_low = [c.astype(low) for c in chances]
        row_dot = [jnp.sum(c * g, axis=0, keepdims=True) for c, g in zip(chances, grad_probs)]
        grad_low = [(c * (g - r) * SCALE).astype(low) for c, g, r in zip(chances, grad_probs, row_dot)]
        value_part = [dot(c, d, (1, 0)).astype(low) for c, d in zip(chances_low, grad)]
        key_part = [dot(g, q, (1, 0)).astype(low) for g, q in zip(grad_low, query)]
        for at, g in enumerate(side):
            probs[g] = chances_low[at]
            scores_grad[g] = grad_low[at]
            block_grads[g, :, :GROUP] = key_part[at].reshape(per_group, GROUP, cols)
            block_grads[g, :, GROUP:] = value_part[at].reshape(per_group, GROUP, cols)
        for g in side:
            for j in range(per_group):
                slot = source[g * per_group + j]
                pltpu.make_async_copy(block_grads.at[g, j], send.at[slot], out_sem).start()
    pltpu.make_async_copy(block_grads, block_grads, out_sem).wait()


def token_kernel(source, probs, scores_grad, slots, attended, query_grad, blocks, in_sems):
    gather(source, slots, blocks, in_sems)
    for group in range(blocks.shape[0]):
        pltpu.make_async_copy(blocks.at[group], blocks.at[group], in_sems.at[group]).wait()
        rows = slice(group * GROUP, (group + 1) * GROUP)
        mixed = dot(probs[group], half(blocks, group, 1), (0, 0)).astype(jnp.bfloat16)
        query_part = dot(scores_grad[group], half(blocks, group, 0), (0, 0)).astype(jnp.bfloat16)
        for head in range(attended.shape[1] // HEAD_DIM):
            own = slice(head * GROUP, (head + 1) * GROUP)
            column = slice(head * HEAD_DIM, (head + 1) * HEAD_DIM)
            attended[rows, column] = mixed[own, column]
            query_grad[rows, column] = query_part[own, column]


def shift(value, axis, steps):
    count = lax.axis_size(axis)
    first, last = max(0, -steps), min(count, count - steps)
    return lax.ppermute(value, axis, [(at, at + steps) for at in range(first, last)])


def exchange(slots):
    return lax.all_to_all(slots, "seq", split_axis=0, concat_axis=0, tiled=True)


def local(queries, neighbor_keys, neighbor_values, out_grad, neighbor_source, send_unit):
    tok_rows, cols = queries.shape
    groups, per_group = neighbor_source.shape
    units = neighbor_keys.shape[0] // GROUP
    slots = send_unit.shape[1] * send_unit.shape[2]
    heads, keys = cols // HEAD_DIM, per_group * GROUP
    low = jnp.bfloat16
    table = send_unit.reshape(slots)
    source = neighbor_source.reshape(units)
    slot_shape = jax.ShapeDtypeStruct((slots, PAIR, cols), low)
    unit_shape = jax.ShapeDtypeStruct((units, GROUP, cols), low)
    tok_shape = jax.ShapeDtypeStruct((tok_rows, cols), low)
    prob_shape = jax.ShapeDtypeStruct((groups, keys, heads * GROUP), low)
    slot_bytes = slots * PAIR * cols * 2
    matmul = 2 * groups * keys * heads * GROUP * cols
    sem = pltpu.SemaphoreType.DMA
    blocks = pltpu.VMEM((groups, per_group, PAIR, cols), low)
    staged = pltpu.VMEM((units, PAIR, cols), low)
    group_sems = pltpu.SemaphoreType.DMA((groups,))

    received = exchange(
        call(
            pack_kernel, [SM, HB, HB], HB, pltpu.HBM(slot_shape.shape, low),
            scratch=[
                staged, pltpu.VMEM((PAIR, cols), low),
                pltpu.SemaphoreType.DMA((2, 2)), sem,
            ],
            moved=2 * slot_bytes, vmem=58,
        )(table, neighbor_keys.reshape(unit_shape.shape), neighbor_values.reshape(unit_shape.shape))
    )
    blank = call(
        blank_kernel, [], HB, pltpu.HBM(slot_shape.shape, low),
        scratch=[pltpu.VMEM((8, PAIR, cols), low), sem], moved=slot_bytes,
    )()

    edge = GROUP - 1
    ahead = shift(jnp.stack([queries[:GROUP], out_grad[:GROUP]]), "seq", -1)
    group_queries = jnp.concatenate([queries[edge:], ahead[0, :edge]], axis=0)
    group_grads = jnp.concatenate([out_grad[edge:], ahead[1, :edge]], axis=0)
    fills = table[None, :] == jnp.arange(units, dtype=jnp.int32)[:, None]
    which = jnp.max(jnp.where(fills, jnp.arange(slots, dtype=jnp.int32)[None, :], -1), axis=1)

    send, probs, scores_grad = call(
        block_kernel, [SM, VM, VM, HB, HB], (HB, VM, VM), (pltpu.HBM(slot_shape.shape, low), prob_shape, prob_shape),
        scratch=[blocks, blocks, group_sems, sem],
        flops=4 * matmul, moved=slot_bytes, aliases={4: 0}, vmem=58,
    )(source, group_queries, group_grads, received, blank)
    returned = exchange(send)

    mixed, query_part = call(
        token_kernel, [SM, VM, VM, HB], (VM, VM), (tok_shape, tok_shape),
        scratch=[blocks, group_sems], flops=2 * matmul, moved=slot_bytes,
    )(source, probs, scores_grad, received)
    behind = shift(jnp.stack([mixed[-GROUP:], query_part[-GROUP:]]), "seq", 1)
    attended = jnp.concatenate([behind[0, 1:], mixed[: tok_rows - edge]], axis=0)
    query_grad = jnp.concatenate([behind[1, 1:], query_part[: tok_rows - edge]], axis=0)

    unit_out = pltpu.HBM(unit_shape.shape, low)
    key_grad, value_grad = call(
        unpack_kernel, [SM, HB], (HB, HB), (unit_out, unit_out),
        scratch=[staged, pltpu.VMEM((PAIR, cols), low), pltpu.SemaphoreType.DMA((4,)), sem, sem],
        moved=slot_bytes, vmem=58,
    )(which, returned)
    flat = (units * GROUP, cols)
    return (attended, query_grad, key_grad.reshape(flat), value_grad.reshape(flat))


def solution(mesh):
    return jax.shard_map(
        local,
        mesh=mesh,
        in_specs=(
            P("seq", "mp"),
            P("seq", "mp"),
            P("seq", "mp"),
            P("seq", "mp"),
            P("seq", None),
            P("seq", None, None),
        ),
        out_specs=(P("seq", "mp"), P("seq", "mp"), P("seq", "mp"), P("seq", "mp")),
        check_vma=False,
    )
```

```python
import jax
import jax.numpy as jnp
from jax import lax
from jax.experimental import pallas as pl
from jax.experimental.pallas import tpu as pltpu
from jax.sharding import PartitionSpec as P

HEAD_DIM = 128
GROUP = 64
PAIR = 2 * GROUP
MIB = 1024 * 1024
SCALE = HEAD_DIM ** (-0.5)
SIDE = 3

VM = pl.BlockSpec(memory_space=pltpu.VMEM)
SM = pl.BlockSpec(memory_space=pltpu.SMEM)
HB = pl.BlockSpec(memory_space=pltpu.HBM)


def call(kernel, in_specs, out_specs, out_shape, scratch=(), flops=0, moved=0, aliases=None, vmem=12):
    return pl.pallas_call(
        kernel,
        out_shape=out_shape,
        in_specs=in_specs,
        out_specs=out_specs,
        scratch_shapes=list(scratch),
        input_output_aliases=aliases or {},
        compiler_params=pltpu.CompilerParams(vmem_limit_bytes=vmem * MIB),
        cost_estimate=pl.CostEstimate(flops=flops, bytes_accessed=moved, transcendentals=0),
    )


def blank_kernel(slots, zeros, sem):
    zeros[...] = jnp.zeros(zeros.shape, zeros.dtype)
    many = zeros.shape[0]
    for first in range(0, slots.shape[0], many):
        pltpu.make_async_copy(zeros, slots.at[pl.ds(first, many)], sem).start()
    pltpu.make_async_copy(slots, slots, sem).wait()


def pack_kernel(table, keys, values, slots, staged, zeros, in_sems, out_sem):
    parts = in_sems.shape[0]
    some = keys.shape[0] // parts
    loads = []
    for part in range(parts):
        own = pl.ds(part * some, some)
        loads.append(pltpu.make_async_copy(keys.at[own], staged.at[own, pl.ds(0, GROUP)], in_sems.at[part, 0]))
        loads.append(pltpu.make_async_copy(values.at[own], staged.at[own, pl.ds(GROUP, GROUP)], in_sems.at[part, 1]))
    for load in loads:
        load.start()
    zeros[...] = jnp.zeros(zeros.shape, zeros.dtype)
    for slot in range(slots.shape[0]):

        @pl.when(table[slot] < 0)
        def _():
            pltpu.make_async_copy(zeros, slots.at[slot], out_sem).start()

    for load in loads:
        load.wait()
    for slot in range(slots.shape[0]):
        unit = table[slot]

        @pl.when(unit >= 0)
        def _():
            pltpu.make_async_copy(staged.at[unit], slots.at[slot], out_sem).start()

    pltpu.make_async_copy(slots, slots, out_sem).wait()


def unpack_kernel(which, slots, keys, values, staged, zeros, in_sems, key_sem, value_sem):
    zeros[...] = jnp.zeros(zeros.shape, zeros.dtype)
    parts = in_sems.shape[0]
    some = keys.shape[0] // parts
    for unit in range(keys.shape[0]):
        slot = which[unit]

        @pl.when(slot >= 0)
        def _():
            pltpu.make_async_copy(slots.at[slot], staged.at[unit], in_sems.at[unit // some]).start()

        @pl.when(slot < 0)
        def _():
            pltpu.make_async_copy(zeros, staged.at[unit], in_sems.at[unit // some]).start()

    for part in range(parts):
        own = pl.ds(part * some, some)
        pltpu.make_async_copy(staged.at[own], staged.at[own], in_sems.at[part]).wait()
        pltpu.make_async_copy(staged.at[own, pl.ds(0, GROUP)], keys.at[own], key_sem).start()
        pltpu.make_async_copy(staged.at[own, pl.ds(GROUP, GROUP)], values.at[own], value_sem).start()
    pltpu.make_async_copy(keys, keys, key_sem).wait()
    pltpu.make_async_copy(values, values, value_sem).wait()


def dot(a, b, contract):
    return lax.dot_general(a, b, ((contract[:1], contract[1:]), ((), ())), preferred_element_type=jnp.float32)


def by_head(rows):
    blank = jnp.zeros((rows.shape[0], HEAD_DIM), rows.dtype)
    heads = rows.shape[1] // HEAD_DIM
    return jnp.concatenate(
        [
            jnp.concatenate(
                [rows[:, h * HEAD_DIM : (h + 1) * HEAD_DIM] if h == at else blank for h in range(heads)], axis=1
            )
            for at in range(heads)
        ],
        axis=0,
    )


def gather(source, slots, blocks, sems):
    groups, per_group = blocks.shape[:2]
    for group in range(groups):
        for j in range(per_group):
            slot = source[group * per_group + j]
            pltpu.make_async_copy(slots.at[slot], blocks.at[group, j], sems.at[group]).start()


def half(blocks, group, part):
    per_group, _, cols = blocks.shape[1:]
    return blocks[group, :, part * GROUP : (part + 1) * GROUP].reshape(per_group * GROUP, cols)


def block_kernel(
    source, queries, grads, slots, blank, send, probs, scores_grad, blocks, block_grads, in_sems, out_sem
):
    groups, per_group, _, cols = blocks.shape
    low = jnp.bfloat16
    gather(source, slots, blocks, in_sems)
    for first in range(0, groups, SIDE):
        side = range(first, min(first + SIDE, groups))
        query = [by_head(queries[g * GROUP : (g + 1) * GROUP]) for g in side]
        grad = [by_head(grads[g * GROUP : (g + 1) * GROUP]) for g in side]
        for g in side:
            pltpu.make_async_copy(blocks.at[g], blocks.at[g], in_sems.at[g]).wait()
        scores = [dot(half(blocks, g, 0), q, (1, 1)) * SCALE for g, q in zip(side, query)]
        grad_probs = [dot(half(blocks, g, 1), d, (1, 1)) for g, d in zip(side, grad)]
        powers = [jnp.exp(s - jnp.max(s, axis=0, keepdims=True)) for s in scores]
        chances = [p * (1.0 / jnp.sum(p, axis=0, keepdims=True)) for p in powers]
        chances_low = [c.astype(low) for c in chances]
        row_dot = [jnp.sum(c * g, axis=0, keepdims=True) for c, g in zip(chances, grad_probs)]
        grad_low = [(c * (g - r) * SCALE).astype(low) for c, g, r in zip(chances, grad_probs, row_dot)]
        value_part = [dot(c, d, (1, 0)).astype(low) for c, d in zip(chances_low, grad)]
        key_part = [dot(g, q, (1, 0)).astype(low) for g, q in zip(grad_low, query)]
        for at, g in enumerate(side):
            probs[g] = chances_low[at]
            scores_grad[g] = grad_low[at]
            block_grads[g, :, :GROUP] = key_part[at].reshape(per_group, GROUP, cols)
            block_grads[g, :, GROUP:] = value_part[at].reshape(per_group, GROUP, cols)
        for g in side:
            for j in range(per_group):
                slot = source[g * per_group + j]
                pltpu.make_async_copy(block_grads.at[g, j], send.at[slot], out_sem).start()
    pltpu.make_async_copy(block_grads, block_grads, out_sem).wait()


def token_kernel(source, probs, scores_grad, slots, attended, query_grad, blocks, in_sems):
    gather(source, slots, blocks, in_sems)
    for group in range(blocks.shape[0]):
        pltpu.make_async_copy(blocks.at[group], blocks.at[group], in_sems.at[group]).wait()
        rows = slice(group * GROUP, (group + 1) * GROUP)
        mixed = dot(probs[group], half(blocks, group, 1), (0, 0)).astype(jnp.bfloat16)
        query_part = dot(scores_grad[group], half(blocks, group, 0), (0, 0)).astype(jnp.bfloat16)
        for head in range(attended.shape[1] // HEAD_DIM):
            own = slice(head * GROUP, (head + 1) * GROUP)
            column = slice(head * HEAD_DIM, (head + 1) * HEAD_DIM)
            attended[rows, column] = mixed[own, column]
            query_grad[rows, column] = query_part[own, column]


def shift(value, axis, steps):
    count = lax.axis_size(axis)
    first, last = max(0, -steps), min(count, count - steps)
    return lax.ppermute(value, axis, [(at, at + steps) for at in range(first, last)])


def exchange(slots):
    return lax.all_to_all(slots, "seq", split_axis=0, concat_axis=0, tiled=True)


def local(queries, neighbor_keys, neighbor_values, out_grad, neighbor_source, send_unit):
    tok_rows, cols = queries.shape
    groups, per_group = neighbor_source.shape
    units = neighbor_keys.shape[0] // GROUP
    slots = send_unit.shape[1] * send_unit.shape[2]
    heads, keys = cols // HEAD_DIM, per_group * GROUP
    low = jnp.bfloat16
    table = send_unit.reshape(slots)
    source = neighbor_source.reshape(units)
    slot_shape = jax.ShapeDtypeStruct((slots, PAIR, cols), low)
    unit_shape = jax.ShapeDtypeStruct((units, GROUP, cols), low)
    tok_shape = jax.ShapeDtypeStruct((tok_rows, cols), low)
    prob_shape = jax.ShapeDtypeStruct((groups, keys, heads * GROUP), low)
    slot_bytes = slots * PAIR * cols * 2
    matmul = 2 * groups * keys * heads * GROUP * cols
    sem = pltpu.SemaphoreType.DMA
    blocks = pltpu.VMEM((groups, per_group, PAIR, cols), low)
    staged = pltpu.VMEM((units, PAIR, cols), low)
    group_sems = pltpu.SemaphoreType.DMA((groups,))

    received = exchange(
        call(
            pack_kernel, [SM, HB, HB], HB, pltpu.HBM(slot_shape.shape, low),
            scratch=[
                staged, pltpu.VMEM((PAIR, cols), low),
                pltpu.SemaphoreType.DMA((2, 2)), sem,
            ],
            moved=2 * slot_bytes, vmem=58,
        )(table, neighbor_keys.reshape(unit_shape.shape), neighbor_values.reshape(unit_shape.shape))
    )
    blank = call(
        blank_kernel, [], HB, pltpu.HBM(slot_shape.shape, low),
        scratch=[pltpu.VMEM((8, PAIR, cols), low), sem], moved=slot_bytes,
    )()

    edge = GROUP - 1
    ahead = shift(jnp.stack([queries[:GROUP], out_grad[:GROUP]]), "seq", -1)
    group_queries = jnp.concatenate([queries[edge:], ahead[0, :edge]], axis=0)
    group_grads = jnp.concatenate([out_grad[edge:], ahead[1, :edge]], axis=0)
    fills = table[None, :] == jnp.arange(units, dtype=jnp.int32)[:, None]
    which = jnp.max(jnp.where(fills, jnp.arange(slots, dtype=jnp.int32)[None, :], -1), axis=1)

    send, probs, scores_grad = call(
        block_kernel, [SM, VM, VM, HB, HB], (HB, VM, VM), (pltpu.HBM(slot_shape.shape, low), prob_shape, prob_shape),
        scratch=[blocks, blocks, group_sems, sem],
        flops=4 * matmul, moved=slot_bytes, aliases={4: 0}, vmem=16,
    )(source, group_queries, group_grads, received, blank)
    returned = exchange(send)

    mixed, query_part = call(
        token_kernel, [SM, VM, VM, HB], (VM, VM), (tok_shape, tok_shape),
        scratch=[blocks, group_sems], flops=2 * matmul, moved=slot_bytes,
    )(source, probs, scores_grad, received)
    behind = shift(jnp.stack([mixed[-GROUP:], query_part[-GROUP:]]), "seq", 1)
    attended = jnp.concatenate([behind[0, 1:], mixed[: tok_rows - edge]], axis=0)
    query_grad = jnp.concatenate([behind[1, 1:], query_part[: tok_rows - edge]], axis=0)

    unit_out = pltpu.HBM(unit_shape.shape, low)
    key_grad, value_grad = call(
        unpack_kernel, [SM, HB], (HB, HB), (unit_out, unit_out),
        scratch=[staged, pltpu.VMEM((PAIR, cols), low), pltpu.SemaphoreType.DMA((4,)), sem, sem],
        moved=slot_bytes, vmem=58,
    )(which, returned)
    flat = (units * GROUP, cols)
    return (attended, query_grad, key_grad.reshape(flat), value_grad.reshape(flat))


def solution(mesh):
    return jax.shard_map(
        local,
        mesh=mesh,
        in_specs=(
            P("seq", "mp"),
            P("seq", "mp"),
            P("seq", "mp"),
            P("seq", "mp"),
            P("seq", None),
            P("seq", None, None),
        ),
        out_specs=(P("seq", "mp"), P("seq", "mp"), P("seq", "mp"), P("seq", "mp")),
        check_vma=False,
    )
```

```python
import functools

import jax
import jax.numpy as jnp
from jax import lax
from jax.experimental import pallas as pl
from jax.experimental.pallas import tpu as pltpu
from jax.sharding import PartitionSpec as P

HEAD_DIM = 128
GROUP = 64
PAIR = 2 * GROUP
MIB = 1024 * 1024
SCALE = HEAD_DIM ** (-0.5)
SIDE = 3
ROWS = 8

VM = pl.BlockSpec(memory_space=pltpu.VMEM)
SM = pl.BlockSpec(memory_space=pltpu.SMEM)
HB = pl.BlockSpec(memory_space=pltpu.HBM)


def call(kernel, in_specs, out_specs, out_shape, scratch=(), flops=0, moved=0, aliases=None, vmem=12):
    return pl.pallas_call(
        kernel,
        out_shape=out_shape,
        in_specs=in_specs,
        out_specs=out_specs,
        scratch_shapes=list(scratch),
        input_output_aliases=aliases or {},
        compiler_params=pltpu.CompilerParams(vmem_limit_bytes=vmem * MIB),
        cost_estimate=pl.CostEstimate(flops=flops, bytes_accessed=moved, transcendentals=0),
    )


def blank_kernel(slots, zeros, sem):
    zeros[...] = jnp.zeros(zeros.shape, zeros.dtype)
    many = zeros.shape[0]
    for first in range(0, slots.shape[0], many):
        pltpu.make_async_copy(zeros, slots.at[pl.ds(first, many)], sem).start()
    pltpu.make_async_copy(slots, slots, sem).wait()


def place(slot, count, cap):
    at, entry = slot // cap, slot % cap
    row = count // ROWS
    y, rest = at // row, at % row
    y = y % (ROWS // 2) * 2 + y // (ROWS // 2)
    return (y * row + rest) * cap + entry


def pack_kernel(count, cap, table, keys, values, slots, staged, zeros, in_sems, out_sem):
    parts = in_sems.shape[0]
    some = keys.shape[0] // parts
    loads = []
    for part in range(parts):
        own = pl.ds(part * some, some)
        loads.append(pltpu.make_async_copy(keys.at[own], staged.at[own, pl.ds(0, GROUP)], in_sems.at[part, 0]))
        loads.append(pltpu.make_async_copy(values.at[own], staged.at[own, pl.ds(GROUP, GROUP)], in_sems.at[part, 1]))
    for load in loads:
        load.start()
    zeros[...] = jnp.zeros(zeros.shape, zeros.dtype)
    for slot in range(slots.shape[0]):

        @pl.when(table[slot] < 0)
        def _():
            pltpu.make_async_copy(zeros, slots.at[place(slot, count, cap)], out_sem).start()

    for load in loads:
        load.wait()
    for slot in range(slots.shape[0]):
        unit = table[slot]

        @pl.when(unit >= 0)
        def _():
            pltpu.make_async_copy(staged.at[unit], slots.at[place(slot, count, cap)], out_sem).start()

    pltpu.make_async_copy(slots, slots, out_sem).wait()


def unpack_kernel(which, slots, keys, values, staged, zeros, in_sems, key_sem, value_sem):
    zeros[...] = jnp.zeros(zeros.shape, zeros.dtype)
    parts = in_sems.shape[0]
    some = keys.shape[0] // parts
    for unit in range(keys.shape[0]):
        slot = which[unit]

        @pl.when(slot >= 0)
        def _():
            pltpu.make_async_copy(slots.at[slot], staged.at[unit], in_sems.at[unit // some]).start()

        @pl.when(slot < 0)
        def _():
            pltpu.make_async_copy(zeros, staged.at[unit], in_sems.at[unit // some]).start()

    for part in range(parts):
        own = pl.ds(part * some, some)
        pltpu.make_async_copy(staged.at[own], staged.at[own], in_sems.at[part]).wait()
        pltpu.make_async_copy(staged.at[own, pl.ds(0, GROUP)], keys.at[own], key_sem).start()
        pltpu.make_async_copy(staged.at[own, pl.ds(GROUP, GROUP)], values.at[own], value_sem).start()
    pltpu.make_async_copy(keys, keys, key_sem).wait()
    pltpu.make_async_copy(values, values, value_sem).wait()


def dot(a, b, contract):
    return lax.dot_general(a, b, ((contract[:1], contract[1:]), ((), ())), preferred_element_type=jnp.float32)


def by_head(rows):
    blank = jnp.zeros((rows.shape[0], HEAD_DIM), rows.dtype)
    heads = rows.shape[1] // HEAD_DIM
    return jnp.concatenate(
        [
            jnp.concatenate(
                [rows[:, h * HEAD_DIM : (h + 1) * HEAD_DIM] if h == at else blank for h in range(heads)], axis=1
            )
            for at in range(heads)
        ],
        axis=0,
    )


def gather(source, slots, blocks, sems):
    groups, per_group = blocks.shape[:2]
    for group in range(groups):
        for j in range(per_group):
            slot = source[group * per_group + j]
            pltpu.make_async_copy(slots.at[slot], blocks.at[group, j], sems.at[group]).start()


def half(blocks, group, part):
    per_group, _, cols = blocks.shape[1:]
    return blocks[group, :, part * GROUP : (part + 1) * GROUP].reshape(per_group * GROUP, cols)


def block_kernel(
    source, queries, grads, slots, blank, send, probs, scores_grad, blocks, block_grads, in_sems, out_sem
):
    groups, per_group, _, cols = blocks.shape
    low = jnp.bfloat16
    gather(source, slots, blocks, in_sems)
    for first in range(0, groups, SIDE):
        side = range(first, min(first + SIDE, groups))
        query = [by_head(queries[g * GROUP : (g + 1) * GROUP]) for g in side]
        grad = [by_head(grads[g * GROUP : (g + 1) * GROUP]) for g in side]
        for g in side:
            pltpu.make_async_copy(blocks.at[g], blocks.at[g], in_sems.at[g]).wait()
        scores = [dot(half(blocks, g, 0), q, (1, 1)) * SCALE for g, q in zip(side, query)]
        grad_probs = [dot(half(blocks, g, 1), d, (1, 1)) for g, d in zip(side, grad)]
        powers = [jnp.exp(s - jnp.max(s, axis=0, keepdims=True)) for s in scores]
        chances = [p * (1.0 / jnp.sum(p, axis=0, keepdims=True)) for p in powers]
        chances_low = [c.astype(low) for c in chances]
        row_dot = [jnp.sum(c * g, axis=0, keepdims=True) for c, g in zip(chances, grad_probs)]
        grad_low = [(c * (g - r) * SCALE).astype(low) for c, g, r in zip(chances, grad_probs, row_dot)]
        value_part = [dot(c, d, (1, 0)).astype(low) for c, d in zip(chances_low, grad)]
        key_part = [dot(g, q, (1, 0)).astype(low) for g, q in zip(grad_low, query)]
        for at, g in enumerate(side):
            probs[g] = chances_low[at]
            scores_grad[g] = grad_low[at]
            block_grads[g, :, :GROUP] = key_part[at].reshape(per_group, GROUP, cols)
            block_grads[g, :, GROUP:] = value_part[at].reshape(per_group, GROUP, cols)
        for g in side:
            for j in range(per_group):
                slot = source[g * per_group + j]
                pltpu.make_async_copy(block_grads.at[g, j], send.at[slot], out_sem).start()
    pltpu.make_async_copy(block_grads, block_grads, out_sem).wait()


def token_kernel(source, probs, scores_grad, slots, attended, query_grad, blocks, in_sems):
    gather(source, slots, blocks, in_sems)
    for group in range(blocks.shape[0]):
        pltpu.make_async_copy(blocks.at[group], blocks.at[group], in_sems.at[group]).wait()
        rows = slice(group * GROUP, (group + 1) * GROUP)
        mixed = dot(probs[group], half(blocks, group, 1), (0, 0)).astype(jnp.bfloat16)
        query_part = dot(scores_grad[group], half(blocks, group, 0), (0, 0)).astype(jnp.bfloat16)
        for head in range(attended.shape[1] // HEAD_DIM):
            own = slice(head * GROUP, (head + 1) * GROUP)
            column = slice(head * HEAD_DIM, (head + 1) * HEAD_DIM)
            attended[rows, column] = mixed[own, column]
            query_grad[rows, column] = query_part[own, column]


def shift(value, axis, steps):
    count = lax.axis_size(axis)
    first, last = max(0, -steps), min(count, count - steps)
    return lax.ppermute(value, axis, [(at, at + steps) for at in range(first, last)])


def exchange(slots):
    count = lax.axis_size("seq")
    order = sorted(range(count), key=lambda at: place(at, count, 1))
    return lax.all_to_all(slots, "seq", split_axis=0, concat_axis=0, tiled=True, axis_index_groups=[order])


def local(queries, neighbor_keys, neighbor_values, out_grad, neighbor_source, send_unit):
    tok_rows, cols = queries.shape
    groups, per_group = neighbor_source.shape
    units = neighbor_keys.shape[0] // GROUP
    count, cap = send_unit.shape[1:]
    slots = count * cap
    heads, keys = cols // HEAD_DIM, per_group * GROUP
    low = jnp.bfloat16
    table = send_unit.reshape(slots)
    source = place(neighbor_source.reshape(units), count, cap)
    slot_shape = jax.ShapeDtypeStruct((slots, PAIR, cols), low)
    unit_shape = jax.ShapeDtypeStruct((units, GROUP, cols), low)
    tok_shape = jax.ShapeDtypeStruct((tok_rows, cols), low)
    prob_shape = jax.ShapeDtypeStruct((groups, keys, heads * GROUP), low)
    slot_bytes = slots * PAIR * cols * 2
    matmul = 2 * groups * keys * heads * GROUP * cols
    sem = pltpu.SemaphoreType.DMA
    blocks = pltpu.VMEM((groups, per_group, PAIR, cols), low)
    staged = pltpu.VMEM((units, PAIR, cols), low)
    group_sems = pltpu.SemaphoreType.DMA((groups,))

    received = exchange(
        call(
            functools.partial(pack_kernel, count, cap), [SM, HB, HB], HB, pltpu.HBM(slot_shape.shape, low),
            scratch=[
                staged, pltpu.VMEM((PAIR, cols), low),
                pltpu.SemaphoreType.DMA((2, 2)), sem,
            ],
            moved=2 * slot_bytes, vmem=58,
        )(table, neighbor_keys.reshape(unit_shape.shape), neighbor_values.reshape(unit_shape.shape))
    )
    blank = call(
        blank_kernel, [], HB, pltpu.HBM(slot_shape.shape, low),
        scratch=[pltpu.VMEM((8, PAIR, cols), low), sem], moved=slot_bytes,
    )()

    edge = GROUP - 1
    ahead = shift(jnp.stack([queries[:GROUP], out_grad[:GROUP]]), "seq", -1)
    group_queries = jnp.concatenate([queries[edge:], ahead[0, :edge]], axis=0)
    group_grads = jnp.concatenate([out_grad[edge:], ahead[1, :edge]], axis=0)
    fills = table[None, :] == jnp.arange(units, dtype=jnp.int32)[:, None]
    which = jnp.max(jnp.where(fills, place(jnp.arange(slots, dtype=jnp.int32), count, cap)[None, :], -1), axis=1)

    send, probs, scores_grad = call(
        block_kernel, [SM, VM, VM, HB, HB], (HB, VM, VM), (pltpu.HBM(slot_shape.shape, low), prob_shape, prob_shape),
        scratch=[blocks, blocks, group_sems, sem],
        flops=4 * matmul, moved=slot_bytes, aliases={4: 0}, vmem=16,
    )(source, group_queries, group_grads, received, blank)
    returned = exchange(send)

    mixed, query_part = call(
        token_kernel, [SM, VM, VM, HB], (VM, VM), (tok_shape, tok_shape),
        scratch=[blocks, group_sems], flops=2 * matmul, moved=slot_bytes,
    )(source, probs, scores_grad, received)
    behind = shift(jnp.stack([mixed[-GROUP:], query_part[-GROUP:]]), "seq", 1)
    attended = jnp.concatenate([behind[0, 1:], mixed[: tok_rows - edge]], axis=0)
    query_grad = jnp.concatenate([behind[1, 1:], query_part[: tok_rows - edge]], axis=0)

    unit_out = pltpu.HBM(unit_shape.shape, low)
    key_grad, value_grad = call(
        unpack_kernel, [SM, HB], (HB, HB), (unit_out, unit_out),
        scratch=[staged, pltpu.VMEM((PAIR, cols), low), pltpu.SemaphoreType.DMA((4,)), sem, sem],
        moved=slot_bytes, vmem=58,
    )(which, returned)
    flat = (units * GROUP, cols)
    return (attended, query_grad, key_grad.reshape(flat), value_grad.reshape(flat))


def solution(mesh):
    return jax.shard_map(
        local,
        mesh=mesh,
        in_specs=(
            P("seq", "mp"),
            P("seq", "mp"),
            P("seq", "mp"),
            P("seq", "mp"),
            P("seq", None),
            P("seq", None, None),
        ),
        out_specs=(P("seq", "mp"), P("seq", "mp"), P("seq", "mp"), P("seq", "mp")),
        check_vma=False,
    )
```

```python
import functools

import jax
import jax.numpy as jnp
from jax import lax
from jax.experimental import pallas as pl
from jax.experimental.pallas import tpu as pltpu
from jax.sharding import PartitionSpec as P

HEAD_DIM = 128
GROUP = 64
PAIR = 2 * GROUP
MIB = 1024 * 1024
SCALE = HEAD_DIM ** (-0.5)
SIDE = 3
ROWS = 8

VM = pl.BlockSpec(memory_space=pltpu.VMEM)
SM = pl.BlockSpec(memory_space=pltpu.SMEM)
HB = pl.BlockSpec(memory_space=pltpu.HBM)


def call(kernel, in_specs, out_specs, out_shape, scratch=(), flops=0, moved=0, aliases=None, vmem=12):
    return pl.pallas_call(
        kernel,
        out_shape=out_shape,
        in_specs=in_specs,
        out_specs=out_specs,
        scratch_shapes=list(scratch),
        input_output_aliases=aliases or {},
        compiler_params=pltpu.CompilerParams(vmem_limit_bytes=vmem * MIB),
        cost_estimate=pl.CostEstimate(flops=flops, bytes_accessed=moved, transcendentals=0),
    )


def blank_kernel(slots, zeros, sem):
    zeros[...] = jnp.zeros(zeros.shape, zeros.dtype)
    many = zeros.shape[0]
    for first in range(0, slots.shape[0], many):
        pltpu.make_async_copy(zeros, slots.at[pl.ds(first, many)], sem).start()
    pltpu.make_async_copy(slots, slots, sem).wait()


def place(slot, count, cap):
    at, entry = slot // cap, slot % cap
    row = count // ROWS
    y, rest = at // row, at % row
    y = y % (ROWS // 2) * 2 + y // (ROWS // 2)
    return (y * row + rest) * cap + entry


def pack_kernel(count, cap, table, keys, values, slots, staged, zeros, in_sems, out_sem):
    parts = in_sems.shape[0]
    some = keys.shape[0] // parts
    loads = []
    for part in range(parts):
        own = pl.ds(part * some, some)
        loads.append(pltpu.make_async_copy(keys.at[own], staged.at[own, pl.ds(0, GROUP)], in_sems.at[part, 0]))
        loads.append(pltpu.make_async_copy(values.at[own], staged.at[own, pl.ds(GROUP, GROUP)], in_sems.at[part, 1]))
    for load in loads:
        load.start()
    zeros[...] = jnp.zeros(zeros.shape, zeros.dtype)
    for slot in range(slots.shape[0]):

        @pl.when(table[slot] < 0)
        def _():
            pltpu.make_async_copy(zeros, slots.at[place(slot, count, cap)], out_sem).start()

    for load in loads:
        load.wait()
    for slot in range(slots.shape[0]):
        unit = table[slot]

        @pl.when(unit >= 0)
        def _():
            pltpu.make_async_copy(staged.at[unit], slots.at[place(slot, count, cap)], out_sem).start()

    pltpu.make_async_copy(slots, slots, out_sem).wait()


def unpack_kernel(which, slots, keys, values, staged, zeros, in_sems, key_sem, value_sem):
    zeros[...] = jnp.zeros(zeros.shape, zeros.dtype)
    parts = in_sems.shape[0]
    some = keys.shape[0] // parts
    for unit in range(keys.shape[0]):
        slot = which[unit]

        @pl.when(slot >= 0)
        def _():
            pltpu.make_async_copy(slots.at[slot], staged.at[unit], in_sems.at[unit // some]).start()

        @pl.when(slot < 0)
        def _():
            pltpu.make_async_copy(zeros, staged.at[unit], in_sems.at[unit // some]).start()

    for part in range(parts):
        own = pl.ds(part * some, some)
        pltpu.make_async_copy(staged.at[own], staged.at[own], in_sems.at[part]).wait()
        pltpu.make_async_copy(staged.at[own, pl.ds(0, GROUP)], keys.at[own], key_sem).start()
        pltpu.make_async_copy(staged.at[own, pl.ds(GROUP, GROUP)], values.at[own], value_sem).start()
    pltpu.make_async_copy(keys, keys, key_sem).wait()
    pltpu.make_async_copy(values, values, value_sem).wait()


def dot(a, b, contract):
    return lax.dot_general(a, b, ((contract[:1], contract[1:]), ((), ())), preferred_element_type=jnp.float32)


def by_head(rows):
    blank = jnp.zeros((rows.shape[0], HEAD_DIM), rows.dtype)
    heads = rows.shape[1] // HEAD_DIM
    return jnp.concatenate(
        [
            jnp.concatenate(
                [rows[:, h * HEAD_DIM : (h + 1) * HEAD_DIM] if h == at else blank for h in range(heads)], axis=1
            )
            for at in range(heads)
        ],
        axis=0,
    )


def gather(source, slots, blocks, sems):
    groups, per_group = blocks.shape[:2]
    for group in range(groups):
        for j in range(per_group):
            slot = source[group * per_group + j]
            pltpu.make_async_copy(slots.at[slot], blocks.at[group, j], sems.at[group]).start()


def half(blocks, group, part):
    per_group, _, cols = blocks.shape[1:]
    return blocks[group, :, part * GROUP : (part + 1) * GROUP].reshape(per_group * GROUP, cols)


def block_kernel(
    source, queries, grads, slots, blank, send, probs, scores_grad, blocks, block_grads, in_sems, out_sem
):
    groups, per_group, _, cols = blocks.shape
    low = jnp.bfloat16
    gather(source, slots, blocks, in_sems)
    for first in range(0, groups, SIDE):
        side = range(first, min(first + SIDE, groups))
        query = [by_head(queries[g * GROUP : (g + 1) * GROUP]) for g in side]
        grad = [by_head(grads[g * GROUP : (g + 1) * GROUP]) for g in side]
        for g in side:
            pltpu.make_async_copy(blocks.at[g], blocks.at[g], in_sems.at[g]).wait()
        scores = [dot(half(blocks, g, 0), q, (1, 1)) * SCALE for g, q in zip(side, query)]
        grad_probs = [dot(half(blocks, g, 1), d, (1, 1)) for g, d in zip(side, grad)]
        powers = [jnp.exp(s - jnp.max(s, axis=0, keepdims=True)) for s in scores]
        chances = [p * (1.0 / jnp.sum(p, axis=0, keepdims=True)) for p in powers]
        chances_low = [c.astype(low) for c in chances]
        row_dot = [jnp.sum(c * g, axis=0, keepdims=True) for c, g in zip(chances, grad_probs)]
        grad_low = [(c * (g - r) * SCALE).astype(low) for c, g, r in zip(chances, grad_probs, row_dot)]
        value_part = [dot(c, d, (1, 0)).astype(low) for c, d in zip(chances_low, grad)]
        key_part = [dot(g, q, (1, 0)).astype(low) for g, q in zip(grad_low, query)]
        for at, g in enumerate(side):
            probs[g] = chances_low[at]
            scores_grad[g] = grad_low[at]
            block_grads[g, :, :GROUP] = key_part[at].reshape(per_group, GROUP, cols)
            block_grads[g, :, GROUP:] = value_part[at].reshape(per_group, GROUP, cols)
        for g in side:
            for j in range(per_group):
                slot = source[g * per_group + j]
                pltpu.make_async_copy(block_grads.at[g, j], send.at[slot], out_sem).start()
    pltpu.make_async_copy(block_grads, block_grads, out_sem).wait()


def token_kernel(source, probs, scores_grad, slots, attended, query_grad, blocks, in_sems):
    gather(source, slots, blocks, in_sems)
    for group in range(blocks.shape[0]):
        pltpu.make_async_copy(blocks.at[group], blocks.at[group], in_sems.at[group]).wait()
        rows = slice(group * GROUP, (group + 1) * GROUP)
        mixed = dot(probs[group], half(blocks, group, 1), (0, 0)).astype(jnp.bfloat16)
        query_part = dot(scores_grad[group], half(blocks, group, 0), (0, 0)).astype(jnp.bfloat16)
        for head in range(attended.shape[1] // HEAD_DIM):
            own = slice(head * GROUP, (head + 1) * GROUP)
            column = slice(head * HEAD_DIM, (head + 1) * HEAD_DIM)
            attended[rows, column] = mixed[own, column]
            query_grad[rows, column] = query_part[own, column]


def shift(value, axis, steps):
    count = lax.axis_size(axis)
    first, last = max(0, -steps), min(count, count - steps)
    return lax.ppermute(value, axis, [(at, at + steps) for at in range(first, last)])


def exchange(slots):
    count = lax.axis_size("seq")
    order = sorted(range(count), key=lambda at: place(at, count, 1))
    return lax.all_to_all(slots, "seq", split_axis=0, concat_axis=0, tiled=True, axis_index_groups=[order])


def local(queries, neighbor_keys, neighbor_values, out_grad, neighbor_source, send_unit):
    tok_rows, cols = queries.shape
    groups, per_group = neighbor_source.shape
    units = neighbor_keys.shape[0] // GROUP
    count, cap = send_unit.shape[1:]
    slots = count * cap
    heads, keys = cols // HEAD_DIM, per_group * GROUP
    low = jnp.bfloat16
    table = send_unit.reshape(slots)
    source = place(neighbor_source.reshape(units), count, cap)
    slot_shape = jax.ShapeDtypeStruct((slots, PAIR, cols), low)
    unit_shape = jax.ShapeDtypeStruct((units, GROUP, cols), low)
    tok_shape = jax.ShapeDtypeStruct((tok_rows, cols), low)
    prob_shape = jax.ShapeDtypeStruct((groups, keys, heads * GROUP), low)
    slot_bytes = slots * PAIR * cols * 2
    matmul = 2 * groups * keys * heads * GROUP * cols
    sem = pltpu.SemaphoreType.DMA
    blocks = pltpu.VMEM((groups, per_group, PAIR, cols), low)
    staged = pltpu.VMEM((units, PAIR, cols), low)
    group_sems = pltpu.SemaphoreType.DMA((groups,))

    received = exchange(
        call(
            functools.partial(pack_kernel, count, cap), [SM, HB, HB], HB, pltpu.HBM(slot_shape.shape, low),
            scratch=[
                staged, pltpu.VMEM((PAIR, cols), low),
                pltpu.SemaphoreType.DMA((2, 2)), sem,
            ],
            moved=2 * slot_bytes, vmem=58,
        )(table, neighbor_keys.reshape(unit_shape.shape), neighbor_values.reshape(unit_shape.shape))
    )
    blank = call(
        blank_kernel, [], HB, pltpu.HBM(slot_shape.shape, low),
        scratch=[pltpu.VMEM((8, PAIR, cols), low), sem], moved=slot_bytes,
    )()

    edge = GROUP - 1
    ahead = shift(jnp.stack([queries[:GROUP], out_grad[:GROUP]]), "seq", -1)
    group_queries = jnp.concatenate([queries[edge:], ahead[0, :edge]], axis=0)
    group_grads = jnp.concatenate([out_grad[edge:], ahead[1, :edge]], axis=0)
    fills = table[None, :] == jnp.arange(units, dtype=jnp.int32)[:, None]
    which = jnp.max(jnp.where(fills, place(jnp.arange(slots, dtype=jnp.int32), count, cap)[None, :], -1), axis=1)

    send, probs, scores_grad = call(
        block_kernel, [SM, VM, VM, HB, HB], (HB, VM, VM), (pltpu.HBM(slot_shape.shape, low), prob_shape, prob_shape),
        scratch=[blocks, blocks, group_sems, sem],
        flops=4 * matmul, moved=slot_bytes, aliases={4: 0}, vmem=16,
    )(source, group_queries, group_grads, received, blank)
    returned = exchange(send)

    mixed, query_part = call(
        token_kernel, [SM, VM, VM, HB], (VM, VM), (tok_shape, tok_shape),
        scratch=[blocks, group_sems], flops=2 * matmul, moved=slot_bytes,
    )(source, probs, scores_grad, received)
    behind = shift(jnp.stack([mixed[-GROUP:], query_part[-GROUP:]]), "seq", 1)
    attended = jnp.concatenate([behind[0, 1:], mixed[: tok_rows - edge]], axis=0)
    query_grad = jnp.concatenate([behind[1, 1:], query_part[: tok_rows - edge]], axis=0)

    unit_out = pltpu.HBM(unit_shape.shape, low)
    key_grad, value_grad = call(
        unpack_kernel, [SM, HB], (HB, HB), (unit_out, unit_out),
        scratch=[staged, pltpu.VMEM((PAIR, cols), low), pltpu.SemaphoreType.DMA((4,)), sem, sem],
        moved=slot_bytes, vmem=8,
    )(which, returned)
    flat = (units * GROUP, cols)
    return (attended, query_grad, key_grad.reshape(flat), value_grad.reshape(flat))


def solution(mesh):
    return jax.shard_map(
        local,
        mesh=mesh,
        in_specs=(
            P("seq", "mp"),
            P("seq", "mp"),
            P("seq", "mp"),
            P("seq", "mp"),
            P("seq", None),
            P("seq", None, None),
        ),
        out_specs=(P("seq", "mp"), P("seq", "mp"), P("seq", "mp"), P("seq", "mp")),
        check_vma=False,
    )
```
